32 devices in a mesh: rep: 4 (over y, x), node: 2 (over core), local: 4 (over z).
Axes of the slice: x: 2, y: 2, z: 4, core: 2. Of those that a mesh axis runs over, the one named last changes fastest.
Arguments:
- inputs: bfloat16 [64, 10240], P(('node', 'local'), 'rep'), may hold values from -6 to 6
- out_grad: bfloat16 [64, 10240], P(('node', 'local'), 'rep'), may hold values from -6 to 6
- w_in: bfloat16 [10240, 20480], P('rep', ('node', 'local')), may hold values from -0.0625 to 0.0625
- w_out: bfloat16 [20480, 10240], P(('node', 'local'), 'rep'), may hold values from -0.0390625 to 0.0390625
Outputs:
- grad_w_in: float32 [10240, 20480], P('rep', ('node', 'local'))
- grad_w_out: float32 [20480, 10240], P(('node', 'local'), 'rep')
- in_grad: bfloat16 [64, 10240], P(('node', 'local'), 'rep')
The draws below stay inside these ranges and needn't reach their ends.
All inputs are finite; a program needn't handle non-finite values.
Results may differ from the reference program's by a relative error of at most 0.0049.
Values may be sent and summed in bfloat16 or wider, within the bound.
A program may use at most 128 MiB of HBM per device.

```python
import jax
import jax.numpy as jnp
from jax import lax

D = 10240
H = 20480
TOKENS = 64


def steps_of(rng, dims, cuts, least, largest):
    def one(position, shards_of):
        steps = jax.random.uniform(jax.random.fold_in(jax.random.fold_in(rng, 6), position), (shards_of,), jnp.float32, least / len(cuts), largest / len(cuts))
        return jnp.repeat(jnp.exp(steps), dims[position] // shards_of).reshape((-1,) + (1,) * (len(dims) - position - 1))

    level = one(*cuts[0])
    for cut in cuts[1:]:
        level = level * one(*cut)
    return level


def centred(rng, extent, deviation, most, split=(), kind=jnp.bfloat16):
    result = deviation * jax.random.normal(rng, extent, jnp.float32)
    if split:
        result = result * steps_of(rng, extent, split, -0.22, 0.18)
    return jnp.clip(result, -most, most).astype(kind)


def setup_inputs(seed: int = 0) -> dict:
    arg_keys = jax.random.split(jax.random.key(seed), 5)
    return {
        "inputs": centred(arg_keys[0], (TOKENS, D), 1.0, 6.0, ((0, 8), (1, 4))),
        "out_grad": centred(arg_keys[1], (TOKENS, D), 1.0, 6.0, ((0, 8), (1, 4))),
        "w_in": centred(arg_keys[2], (D, H), D ** -0.5, 0.0625, ((0, 4), (1, 8))),
        "w_out": centred(arg_keys[3], (H, D), H ** -0.5, 0.0390625, ((0, 8), (1, 4))),
    }


def gelu_tanh(value):
    return jax.nn.gelu(value, approximate=True)

def reference(inputs, out_grad, w_in, w_out):
    pre = jnp.dot(inputs, w_in, preferred_element_type=jnp.float32)
    act, back = jax.vjp(gelu_tanh, pre)
    act = act.astype(jnp.bfloat16)
    act_grad = lax.dot_general(out_grad, w_out, (((1,), (1,)), ((), ())), preferred_element_type=jnp.float32)
    pre_grad = back(act_grad)[0].astype(jnp.bfloat16)
    in_grad = lax.dot_general(pre_grad, w_in, (((1,), (1,)), ((), ())), preferred_element_type=jnp.float32).astype(jnp.bfloat16)
    factor = jnp.float32(TOKENS) ** (-0.5)
    grad_in = lax.dot_general(inputs, pre_grad, (((0,), (0,)), ((), ())), preferred_element_type=jnp.float32) * factor
    grad_out = lax.dot_general(act, out_grad, (((0,), (0,)), ((), ())), preferred_element_type=jnp.float32) * factor
    return (grad_in, grad_out, in_grad)
```

```python
import functools

import jax
import jax.numpy as jnp
from jax import lax
from jax.experimental import pallas as pl
from jax.experimental.pallas import tpu as pltpu
from jax.sharding import PartitionSpec as P

MESH = pl.DeviceIdType.MESH
F32, BF16 = jnp.float32, jnp.bfloat16
NT = (((1,), (1,)), ((), ()))
TN = (((0,), (0,)), ((), ()))


def gelu_tanh(value):
    return jax.nn.gelu(value, approximate=True)


def activate(pre, act_grad):
    act, back = jax.vjp(gelu_tanh, pre)
    pre_grad = back(act_grad)[0].astype(BF16)
    return (act.astype(BF16), pre_grad)


def gelu_and_slope(x):
    c = 0.7978845608028654
    t = jnp.tanh(c * (x + 0.044715 * (x * x * x)))
    half = 0.5 * (1.0 + t)
    slope = half + 0.5 * x * (1.0 - t * t) * (c * (1.0 + 3 * 0.044715 * (x * x)))
    return x * half, slope


def exchange(
    R, N, L, wc,
    x_hbm, g_hbm, w1_hbm, w2_hbm,
    rows_x, rows_g, act_o, pg_o, in_o,
    w1, w2, own, gat, stage, part_s, part_r, ap, pgp, fpart, qpart, qrow, srow, rrow,
    w_sem, own_sem, z_send, z_recv, c_send, c_recv, r_send, r_recv, a_send, a_recv,
    h_send, h_recv, s_send, s_recv,
):
    rep, node, loc = lax.axis_index("rep"), lax.axis_index("node"), lax.axis_index("local")
    G = N * L
    b, d = x_hbm.shape
    h = w1_hbm.shape[1]
    T = G * b
    rr = T // R
    other = 1 - node
    n1 = d // wc

    w1c, w2c = [], []
    for i in range(n1):
        cp = pltpu.make_async_copy(w1_hbm.at[pl.ds(i * wc, wc)], w1.at[pl.ds(i * wc, wc)], w_sem.at[0, i])
        w1c.append(cp)
    for i in range(h // wc):
        cp = pltpu.make_async_copy(w2_hbm.at[pl.ds(i * wc, wc)], w2.at[pl.ds(i * wc, wc)], w_sem.at[1, i])
        w2c.append(cp)
    oc = [
        pltpu.make_async_copy(x_hbm, own.at[0], own_sem.at[0]),
        pltpu.make_async_copy(g_hbm, own.at[1], own_sem.at[1]),
    ]
    for cp in oc + w1c + w2c:
        cp.start()

    barrier = pltpu.get_barrier_semaphore()
    for k in range(1, L):
        pl.semaphore_signal(barrier, inc=1, device_id={"local": lax.rem(loc + k, L)}, device_id_type=MESH)
    pl.semaphore_signal(barrier, inc=1, device_id={"node": other}, device_id_type=MESH)
    for k in range(1, R):
        pl.semaphore_signal(barrier, inc=1, device_id={"rep": lax.rem(rep + k, R)}, device_id_type=MESH)
    pl.semaphore_wait(barrier, (L - 1) + 1 + (R - 1))

    mine = node * L + loc
    sends = []

    def zcopy(a, k):
        to = lax.rem(loc + k, L)
        return pltpu.make_async_remote_copy(
            src_ref=own.at[a], dst_ref=gat.at[a, mine],
            send_sem=z_send.at[a, k], recv_sem=z_recv.at[a, k],
            device_id={"local": to}, device_id_type=MESH)

    def ccopy(a, k, src, slot):
        return pltpu.make_async_remote_copy(
            src_ref=src, dst_ref=gat.at[a, slot],
            send_sem=c_send.at[a, k], recv_sem=c_recv.at[a, k],
            device_id={"node": other}, device_id_type=MESH)

    fwd = [[None] * L for _ in range(2)]
    zs = [[None] * L for _ in range(2)]
    for a in range(2):
        oc[a].wait()
        for k in range(1, L):
            zs[a][k] = zcopy(a, k)
            zs[a][k].start()
        fwd[a][0] = ccopy(a, 0, own.at[a], mine)
        fwd[a][0].start()

    def gather(a):
        for k in range(1, L):
            frm = lax.rem(loc + L - k, L)
            zs[a][k].wait_recv()
            slot = node * L + frm
            fwd[a][k] = ccopy(a, k, gat.at[a, slot], slot)
            fwd[a][k].start()
        for k in range(L):
            fwd[a][k].wait_recv()
        gat[a, mine] = own[a]
        for i in range(G):
            stage[i * b:(i + 1) * b, :] = gat[a, i].astype(F32)
        return stage[...].astype(BF16)

    def rsend(a):
        cps = []
        for k in range(1, R):
            to = lax.rem(rep + k, R)
            cp = pltpu.make_async_remote_copy(
                src_ref=part_s.at[a, to], dst_ref=part_r.at[a, k],
                send_sem=r_send.at[a, k], recv_sem=r_recv.at[a, k],
                device_id={"rep": to}, device_id_type=MESH)
            cp.start()
            cps.append(cp)
        return cps

    rows_x[...] = gather(0)
    for cp in w1c:
        cp.wait()

    @pl.loop(0, h // wc)
    def _(i):
        cols = pl.ds(pl.multiple_of(i * wc, wc), wc)
        p = jnp.dot(rows_x[...], w1[:, cols], preferred_element_type=F32)
        fpart[0, :, cols] = p
        for r in range(R):
            part_s[0, r, :, cols] = p[r * rr:(r + 1) * rr].astype(BF16)

    rs0 = rsend(0)

    rows_g[...] = gather(1)
    for cp in w2c:
        cp.wait()

    @pl.loop(0, h // wc)
    def _(i):
        cols = pl.ds(pl.multiple_of(i * wc, wc), wc)
        p = lax.dot_general(rows_g[...], w2[cols, :], NT, preferred_element_type=F32)
        fpart[1, :, cols] = p
        for r in range(R):
            part_s[1, r, :, cols] = p[r * rr:(r + 1) * rr].astype(BF16)

    rs1 = rsend(1)

    myrows = pl.ds(pl.multiple_of(rep * rr, rr), rr)

    def total(a):
        s = fpart[a, myrows, :]
        for k in range(1, R):
            s = s + part_r[a, k].astype(F32)
        return s

    def asend(a, dst):
        cps = []
        for k in range(1, R):
            to = lax.rem(rep + k, R)
            cp = pltpu.make_async_remote_copy(
                src_ref=ap.at[a], dst_ref=dst.at[rep],
                send_sem=a_send.at[a, k], recv_sem=a_recv.at[a, k],
                device_id={"rep": to}, device_id_type=MESH)
            cp.start()
            cps.append(cp)
        return cps

    for cp in rs0:
        cp.wait_recv()
    act, slope = gelu_and_slope(total(0))
    ap[0] = act.astype(BF16)
    fpart[0, myrows, :] = slope
    for cp in rs1:
        cp.wait_recv()
    ap[1] = (total(1) * fpart[0, myrows, :]).astype(BF16)
    ag_pg = asend(1, pgp.at[1])
    ag_act = asend(0, pgp.at[0])
    pgp[1, rep] = ap[1]
    for cp in ag_pg:
        cp.wait_recv()
    for r in range(R):
        pg_o[r * rr:(r + 1) * rr, :] = pgp[1, r]

    hr = L * b

    @pl.loop(0, d // wc)
    def _(i):
        cols = pl.ds(pl.multiple_of(i * wc, wc), wc)
        qpart[:, cols] = lax.dot_general(pg_o[...], w1[cols, :], NT, preferred_element_type=F32)

    hx = pltpu.make_async_remote_copy(
        src_ref=qpart.at[pl.ds(pl.multiple_of(other * hr, hr), hr)], dst_ref=qrow,
        send_sem=h_send, recv_sem=h_recv, device_id={"node": other}, device_id_type=MESH)
    hx.start()
    hx.wait_recv()
    for l in range(L):
        srow[l] = (
            qpart[pl.ds(pl.multiple_of(node * hr + l * b, b), b), :] + qrow[l * b:(l + 1) * b, :]
        ).astype(BF16)
    ss = []
    for k in range(1, L):
        to = lax.rem(loc + k, L)
        cp = pltpu.make_async_remote_copy(
            src_ref=srow.at[to], dst_ref=rrow.at[k],
            send_sem=s_send.at[k], recv_sem=s_recv.at[k],
            device_id={"local": to}, device_id_type=MESH)
        cp.start()
        ss.append(cp)
    pgp[0, rep] = ap[0]
    for cp in ag_act:
        cp.wait_recv()
    for r in range(R):
        act_o[r * rr:(r + 1) * rr, :] = pgp[0, r]
    off = pl.multiple_of(loc * b, b)
    s = qpart[pl.ds(pl.multiple_of(node * hr + loc * b, b), b), :] + qrow[pl.ds(off, b), :]
    for cp in ss:
        cp.wait_recv()
    for k in range(1, L):
        s = s + rrow[k].astype(F32)
    in_o[...] = s.astype(BF16)
    for a in range(2):
        for k in range(1, L):
            zs[a][k].wait_send()
        for k in range(L):
            fwd[a][k].wait_send()
    for cp in rs0 + rs1 + ag_pg + ag_act + [hx] + ss:
        cp.wait_send()


def weight_grads(factor, x, pg, act, g, o1, o2):
    o1[...] = lax.dot_general(x[...], pg[...], TN, preferred_element_type=F32) * factor
    o2[...] = lax.dot_general(act[...], g[...], TN, preferred_element_type=F32) * factor


def fused(R, N, L, inputs, out_grad, w_in, w_out):
    b, d = inputs.shape
    h = w_in.shape[1]
    G = N * L
    T = G * b
    rr = T // R
    wc = 256
    vm = pl.BlockSpec(memory_space=pltpu.VMEM)
    hbm = pl.BlockSpec(memory_space=pl.ANY)
    dma = pltpu.SemaphoreType.DMA
    rows_x, rows_g, act, pg, ing = pl.pallas_call(
        functools.partial(exchange, R, N, L, wc),
        out_shape=[
            jax.ShapeDtypeStruct((T, d), BF16),
            jax.ShapeDtypeStruct((T, d), BF16),
            jax.ShapeDtypeStruct((T, h), BF16),
            jax.ShapeDtypeStruct((T, h), BF16),
            jax.ShapeDtypeStruct((b, d), BF16),
        ],
        in_specs=[hbm] * 4,
        out_specs=[vm] * 5,
        scratch_shapes=[
            pltpu.VMEM((d, h), BF16),
            pltpu.VMEM((h, d), BF16),
            pltpu.VMEM((2, b, d), BF16),
            pltpu.VMEM((2, G, b, d), BF16),
            pltpu.VMEM((T, d), F32),
            pltpu.VMEM((2, R, rr, h), BF16),
            pltpu.VMEM((2, R, rr, h), BF16),
            pltpu.VMEM((2, rr, h), BF16),
            pltpu.VMEM((2, R, rr, h), BF16),
            pltpu.VMEM((2, T, h), F32),
            pltpu.VMEM((T, d), F32),
            pltpu.VMEM((L * b, d), F32),
            pltpu.VMEM((L, b, d), BF16),
            pltpu.VMEM((L, b, d), BF16),
            dma((2, max(d, h) // wc)),
            dma((2,)),
            dma((2, L)), dma((2, L)),
            dma((2, L)), dma((2, L)),
            dma((2, R)), dma((2, R)),
            dma((2, R)), dma((2, R)),
            dma(()), dma(()),
            dma((L,)), dma((L,)),
        ],
        compiler_params=pltpu.CompilerParams(
            collective_id=0, has_side_effects=True, vmem_limit_bytes=56 * 2**20
        ),
        name="exchange",
    )(inputs, out_grad, w_in, w_out)
    steps = 10
    bd, bh = d // steps, h // steps
    factor = float(T) ** -0.5
    g1, g2 = pl.pallas_call(
        functools.partial(weight_grads, factor),
        grid=(steps,),
        out_shape=[jax.ShapeDtypeStruct((d, h), F32), jax.ShapeDtypeStruct((h, d), F32)],
        in_specs=[
            pl.BlockSpec((T, bd), lambda i: (0, i)),
            pl.BlockSpec((T, h), lambda i: (0, 0)),
            pl.BlockSpec((T, bh), lambda i: (0, i)),
            pl.BlockSpec((T, d), lambda i: (0, 0)),
        ],
        out_specs=[pl.BlockSpec((bd, h), lambda i: (i, 0)), pl.BlockSpec((bh, d), lambda i: (i, 0))],
        compiler_params=pltpu.CompilerParams(vmem_limit_bytes=40 * 2**20),
        name="weight_grads",
    )(rows_x, pg, act, rows_g)
    return g1, g2, ing


def plain(inputs, out_grad, w_in, w_out):
    rows_in, rows_grad = (
        lax.all_gather(inputs, ("node", "local"), axis=0, tiled=True),
        lax.all_gather(out_grad, ("node", "local"), axis=0, tiled=True),
    )
    pre_part = jnp.dot(rows_in, w_in, preferred_element_type=F32)
    grad_part = lax.dot_general(rows_grad, w_out, NT, preferred_element_type=F32)
    pre, act_grad = lax.psum((pre_part, grad_part), "rep")
    act, pre_grad = activate(pre, act_grad)
    factor = jnp.float32(rows_in.shape[0]) ** (-0.5)
    grad_in = lax.dot_general(rows_in, pre_grad, TN, preferred_element_type=F32) * factor
    grad_out = lax.dot_general(act, rows_grad, TN, preferred_element_type=F32) * factor
    input_part = lax.dot_general(pre_grad, w_in, NT, preferred_element_type=F32)
    owned = lax.psum_scatter(input_part, ("node", "local"), scatter_dimension=0, tiled=True)
    return (grad_in, grad_out, owned.astype(BF16))


def local(R, N, L, inputs, out_grad, w_in, w_out):
    b, d = inputs.shape
    h = w_in.shape[1]
    fits = (
        N == 2 and b % 8 == 0 and d % 1280 == 0 and h % 1280 == 0
        and (N * L * b) % (16 * R) == 0 and d * h * 4 <= 28 * 2**20
    )
    if fits:
        return fused(R, N, L, inputs, out_grad, w_in, w_out)
    return plain(inputs, out_grad, w_in, w_out)


def solution(mesh):
    R, N, L = mesh.shape["rep"], mesh.shape["node"], mesh.shape["local"]
    in_specs = (
        P(("node", "local"), "rep"),
        P(("node", "local"), "rep"),
        P("rep", ("node", "local")),
        P(("node", "local"), "rep"),
    )
    out_specs = (
        P("rep", ("node", "local")),
        P(("node", "local"), "rep"),
        P(("node", "local"), "rep"),
    )
    return jax.shard_map(
        functools.partial(local, R, N, L), mesh=mesh, in_specs=in_specs, out_specs=out_specs, check_vma=False
    )
```

```python
import functools

import jax
import jax.numpy as jnp
from jax import lax
from jax.experimental import pallas as pl
from jax.experimental.pallas import tpu as pltpu
from jax.sharding import PartitionSpec as P

MESH = pl.DeviceIdType.MESH
F32, BF16 = jnp.float32, jnp.bfloat16
NT = (((1,), (1,)), ((), ()))
TN = (((0,), (0,)), ((), ()))


def gelu_tanh(value):
    return jax.nn.gelu(value, approximate=True)


def activate(pre, act_grad):
    act, back = jax.vjp(gelu_tanh, pre)
    pre_grad = back(act_grad)[0].astype(BF16)
    return (act.astype(BF16), pre_grad)


def gelu_and_slope(x):
    c = 0.7978845608028654
    t = jnp.tanh(c * (x + 0.044715 * (x * x * x)))
    half = 0.5 * (1.0 + t)
    slope = half + 0.5 * x * (1.0 - t * t) * (c * (1.0 + 3 * 0.044715 * (x * x)))
    return x * half, slope


def exchange(
    R, N, L, wc,
    x_hbm, g_hbm, w1_hbm, w2_hbm,
    rows_x, rows_g, act_o, pg_o, in_o,
    w1, w2, own, gat, stage, part_s, part_r, ap, pgp, fpart, qpart, qrow, srow, rrow,
    w_sem, own_sem, z_send, z_recv, c_send, c_recv, r_send, r_recv, a_send, a_recv,
    h_send, h_recv, s_send, s_recv,
):
    rep, node, loc = lax.axis_index("rep"), lax.axis_index("node"), lax.axis_index("local")
    G = N * L
    b, d = x_hbm.shape
    h = w1_hbm.shape[1]
    T = G * b
    rr = T // R
    other = 1 - node
    n1 = d // wc

    w1c, w2c = [], []
    for i in range(n1):
        cp = pltpu.make_async_copy(w1_hbm.at[pl.ds(i * wc, wc)], w1.at[pl.ds(i * wc, wc)], w_sem.at[0, i])
        w1c.append(cp)
    for i in range(h // wc):
        cp = pltpu.make_async_copy(w2_hbm.at[pl.ds(i * wc, wc)], w2.at[pl.ds(i * wc, wc)], w_sem.at[1, i])
        w2c.append(cp)
    oc = [
        pltpu.make_async_copy(x_hbm, own.at[0], own_sem.at[0]),
        pltpu.make_async_copy(g_hbm, own.at[1], own_sem.at[1]),
    ]
    for cp in oc + w1c[:n1 // 2]:
        cp.start()

    barrier = pltpu.get_barrier_semaphore()
    for k in range(1, L):
        pl.semaphore_signal(barrier, inc=1, device_id={"local": lax.rem(loc + k, L)}, device_id_type=MESH)
    pl.semaphore_signal(barrier, inc=1, device_id={"node": other}, device_id_type=MESH)
    for k in range(1, R):
        pl.semaphore_signal(barrier, inc=1, device_id={"rep": lax.rem(rep + k, R)}, device_id_type=MESH)
    pl.semaphore_wait(barrier, (L - 1) + 1 + (R - 1))

    mine = node * L + loc
    sends = []

    def zcopy(a, k):
        to = lax.rem(loc + k, L)
        return pltpu.make_async_remote_copy(
            src_ref=own.at[a], dst_ref=gat.at[a, mine],
            send_sem=z_send.at[a, k], recv_sem=z_recv.at[a, k],
            device_id={"local": to}, device_id_type=MESH)

    def ccopy(a, k, src, slot):
        return pltpu.make_async_remote_copy(
            src_ref=src, dst_ref=gat.at[a, slot],
            send_sem=c_send.at[a, k], recv_sem=c_recv.at[a, k],
            device_id={"node": other}, device_id_type=MESH)

    fwd = [[None] * L for _ in range(2)]
    zs = [[None] * L for _ in range(2)]

    def spread(a):
        for k in range(1, L):
            zs[a][k] = zcopy(a, k)
            zs[a][k].start()
        fwd[a][0] = ccopy(a, 0, own.at[a], mine)
        fwd[a][0].start()

    for cp in oc:
        cp.wait()
    spread(0)
    for cp in w1c[n1 // 2:]:
        cp.start()

    def gather(a):
        for k in range(1, L):
            frm = lax.rem(loc + L - k, L)
            zs[a][k].wait_recv()
            slot = node * L + frm
            fwd[a][k] = ccopy(a, k, gat.at[a, slot], slot)
            fwd[a][k].start()
        if a == 0:
            spread(1)
            for cp in w2c:
                cp.start()
        for k in range(L):
            fwd[a][k].wait_recv()
        gat[a, mine] = own[a]
        for i in range(G):
            stage[i * b:(i + 1) * b, :] = gat[a, i].astype(F32)
        return stage[...].astype(BF16)

    def rsend(a):
        cps = []
        for k in range(1, R):
            to = lax.rem(rep + k, R)
            cp = pltpu.make_async_remote_copy(
                src_ref=part_s.at[a, to], dst_ref=part_r.at[a, k],
                send_sem=r_send.at[a, k], recv_sem=r_recv.at[a, k],
                device_id={"rep": to}, device_id_type=MESH)
            cp.start()
            cps.append(cp)
        return cps

    rows_x[...] = gather(0)
    for cp in w1c:
        cp.wait()

    @pl.loop(0, h // wc)
    def _(i):
        cols = pl.ds(pl.multiple_of(i * wc, wc), wc)
        p = jnp.dot(rows_x[...], w1[:, cols], preferred_element_type=F32)
        fpart[0, :, cols] = p
        for r in range(R):
            part_s[0, r, :, cols] = p[r * rr:(r + 1) * rr].astype(BF16)

    rs0 = rsend(0)

    rows_g[...] = gather(1)
    @pl.loop(0, h // wc)
    def _(i):
        cols = pl.ds(pl.multiple_of(i * wc, wc), wc)
        pltpu.make_async_copy(w2_hbm.at[cols], w2.at[cols], w_sem.at[1, i]).wait()
        p = lax.dot_general(rows_g[...], w2[cols, :], NT, preferred_element_type=F32)
        fpart[1, :, cols] = p
        for r in range(R):
            part_s[1, r, :, cols] = p[r * rr:(r + 1) * rr].astype(BF16)

    rs1 = rsend(1)

    myrows = pl.ds(pl.multiple_of(rep * rr, rr), rr)

    def total(a):
        s = fpart[a, myrows, :]
        for k in range(1, R):
            s = s + part_r[a, k].astype(F32)
        return s

    def asend(a, dst):
        cps = []
        for k in range(1, R):
            to = lax.rem(rep + k, R)
            cp = pltpu.make_async_remote_copy(
                src_ref=ap.at[a], dst_ref=dst.at[rep],
                send_sem=a_send.at[a, k], recv_sem=a_recv.at[a, k],
                device_id={"rep": to}, device_id_type=MESH)
            cp.start()
            cps.append(cp)
        return cps

    for cp in rs0:
        cp.wait_recv()
    act, slope = gelu_and_slope(total(0))
    ap[0] = act.astype(BF16)
    fpart[0, myrows, :] = slope
    for cp in rs1:
        cp.wait_recv()
    ap[1] = (total(1) * fpart[0, myrows, :]).astype(BF16)
    ag_pg = asend(1, pgp.at[1])
    pgp[1, rep] = ap[1]
    for cp in ag_pg:
        cp.wait_recv()
    for r in range(R):
        pg_o[r * rr:(r + 1) * rr, :] = pgp[1, r]
    ag_act = asend(0, pgp.at[0])

    hr = L * b

    C = h_send.shape[0]
    dc = d // C
    give = pl.ds(pl.multiple_of(other * hr, hr), hr)
    hx, ss = [], []

    def pass_on(c):
        cols = slice(c * dc, (c + 1) * dc)
        hx[c].wait_recv()
        for l in range(L):
            srow[l, :, cols] = (
                qpart[pl.ds(pl.multiple_of(node * hr + l * b, b), b), cols] + qrow[l * b:(l + 1) * b, cols]
            ).astype(BF16)
        for k in range(1, L):
            to = lax.rem(loc + k, L)
            cp = pltpu.make_async_remote_copy(
                src_ref=srow.at[to, :, pl.ds(c * dc, dc)], dst_ref=rrow.at[k, :, pl.ds(c * dc, dc)],
                send_sem=s_send.at[k, c], recv_sem=s_recv.at[k, c],
                device_id={"local": to}, device_id_type=MESH)
            cp.start()
            ss.append(cp)

    for c in range(C):
        cols = slice(c * dc, (c + 1) * dc)
        qpart[:, cols] = lax.dot_general(pg_o[...], w1[cols, :], NT, preferred_element_type=F32)
        cp = pltpu.make_async_remote_copy(
            src_ref=qpart.at[give, pl.ds(c * dc, dc)], dst_ref=qrow.at[:, pl.ds(c * dc, dc)],
            send_sem=h_send.at[c], recv_sem=h_recv.at[c], device_id={"node": other}, device_id_type=MESH)
        cp.start()
        hx.append(cp)
        if c:
            pass_on(c - 1)
    pass_on(C - 1)
    pgp[0, rep] = ap[0]
    for cp in ag_act:
        cp.wait_recv()
    for r in range(R):
        act_o[r * rr:(r + 1) * rr, :] = pgp[0, r]
    off = pl.multiple_of(loc * b, b)
    s = qpart[pl.ds(pl.multiple_of(node * hr + loc * b, b), b), :] + qrow[pl.ds(off, b), :]
    for cp in ss:
        cp.wait_recv()
    for k in range(1, L):
        s = s + rrow[k].astype(F32)
    in_o[...] = s.astype(BF16)
    for a in range(2):
        for k in range(1, L):
            zs[a][k].wait_send()
        for k in range(L):
            fwd[a][k].wait_send()
    for cp in rs0 + rs1 + ag_pg + ag_act + hx + ss:
        cp.wait_send()


def weight_grads(factor, x, pg, act, g, ing, o1, o2, o3):
    o3[...] = ing[...]
    o1[...] = lax.dot_general(x[...], pg[...], TN, preferred_element_type=F32) * factor
    o2[...] = lax.dot_general(act[...], g[...], TN, preferred_element_type=F32) * factor


def fused(R, N, L, inputs, out_grad, w_in, w_out):
    b, d = inputs.shape
    h = w_in.shape[1]
    G = N * L
    T = G * b
    rr = T // R
    wc = 256
    vm = pl.BlockSpec(memory_space=pltpu.VMEM)
    hbm = pl.BlockSpec(memory_space=pl.ANY)
    dma = pltpu.SemaphoreType.DMA
    rows_x, rows_g, act, pg, ing = pl.pallas_call(
        functools.partial(exchange, R, N, L, wc),
        out_shape=[
            jax.ShapeDtypeStruct((T, d), BF16),
            jax.ShapeDtypeStruct((T, d), BF16),
            jax.ShapeDtypeStruct((T, h), BF16),
            jax.ShapeDtypeStruct((T, h), BF16),
            jax.ShapeDtypeStruct((b, d), BF16),
        ],
        in_specs=[hbm] * 4,
        out_specs=[vm] * 5,
        scratch_shapes=[
            pltpu.VMEM((d, h), BF16),
            pltpu.VMEM((h, d), BF16),
            pltpu.VMEM((2, b, d), BF16),
            pltpu.VMEM((2, G, b, d), BF16),
            pltpu.VMEM((T, d), F32),
            pltpu.VMEM((2, R, rr, h), BF16),
            pltpu.VMEM((2, R, rr, h), BF16),
            pltpu.VMEM((2, rr, h), BF16),
            pltpu.VMEM((2, R, rr, h), BF16),
            pltpu.VMEM((2, T, h), F32),
            pltpu.VMEM((T, d), F32),
            pltpu.VMEM((L * b, d), F32),
            pltpu.VMEM((L, b, d), BF16),
            pltpu.VMEM((L, b, d), BF16),
            dma((2, max(d, h) // wc)),
            dma((2,)),
            dma((2, L)), dma((2, L)),
            dma((2, L)), dma((2, L)),
            dma((2, R)), dma((2, R)),
            dma((2, R)), dma((2, R)),
            dma((5,)), dma((5,)),
            dma((L, 5)), dma((L, 5)),
        ],
        compiler_params=pltpu.CompilerParams(
            collective_id=0, has_side_effects=True, vmem_limit_bytes=56 * 2**20
        ),
        name="exchange",
    )(inputs, out_grad, w_in, w_out)
    steps = 10
    bd, bh = d // steps, h // steps
    factor = float(T) ** -0.5
    return pl.pallas_call(
        functools.partial(weight_grads, factor),
        grid=(steps,),
        out_shape=[jax.ShapeDtypeStruct((d, h), F32), jax.ShapeDtypeStruct((h, d), F32),
                   jax.ShapeDtypeStruct((b, d), BF16)],
        in_specs=[
            pl.BlockSpec((T, bd), lambda i: (0, i)),
            pl.BlockSpec((T, h), lambda i: (0, 0)),
            pl.BlockSpec((T, bh), lambda i: (0, i)),
            pl.BlockSpec((T, d), lambda i: (0, 0)),
            pl.BlockSpec((b, d), lambda i: (0, 0)),
        ],
        out_specs=[pl.BlockSpec((bd, h), lambda i: (i, 0)), pl.BlockSpec((bh, d), lambda i: (i, 0)),
                   pl.BlockSpec((b, d), lambda i: (0, 0))],
        compiler_params=pltpu.CompilerParams(vmem_limit_bytes=60 * 2**20),
        name="weight_grads",
    )(rows_x, pg, act, rows_g, ing)


def plain(inputs, out_grad, w_in, w_out):
    rows_in, rows_grad = (
        lax.all_gather(inputs, ("node", "local"), axis=0, tiled=True),
        lax.all_gather(out_grad, ("node", "local"), axis=0, tiled=True),
    )
    pre_part = jnp.dot(rows_in, w_in, preferred_element_type=F32)
    grad_part = lax.dot_general(rows_grad, w_out, NT, preferred_element_type=F32)
    pre, act_grad = lax.psum((pre_part, grad_part), "rep")
    act, pre_grad = activate(pre, act_grad)
    factor = jnp.float32(rows_in.shape[0]) ** (-0.5)
    grad_in = lax.dot_general(rows_in, pre_grad, TN, preferred_element_type=F32) * factor
    grad_out = lax.dot_general(act, rows_grad, TN, preferred_element_type=F32) * factor
    input_part = lax.dot_general(pre_grad, w_in, NT, preferred_element_type=F32)
    owned = lax.psum_scatter(input_part, ("node", "local"), scatter_dimension=0, tiled=True)
    return (grad_in, grad_out, owned.astype(BF16))


def local(R, N, L, inputs, out_grad, w_in, w_out):
    b, d = inputs.shape
    h = w_in.shape[1]
    fits = (
        N == 2 and b % 8 == 0 and d % 1280 == 0 and h % 1280 == 0
        and (N * L * b) % (16 * R) == 0 and d * h * 4 <= 28 * 2**20
    )
    if fits:
        return fused(R, N, L, inputs, out_grad, w_in, w_out)
    return plain(inputs, out_grad, w_in, w_out)


def solution(mesh):
    R, N, L = mesh.shape["rep"], mesh.shape["node"], mesh.shape["local"]
    in_specs = (
        P(("node", "local"), "rep"),
        P(("node", "local"), "rep"),
        P("rep", ("node", "local")),
        P(("node", "local"), "rep"),
    )
    out_specs = (
        P("rep", ("node", "local")),
        P(("node", "local"), "rep"),
        P(("node", "local"), "rep"),
    )
    return jax.shard_map(
        functools.partial(local, R, N, L), mesh=mesh, in_specs=in_specs, out_specs=out_specs, check_vma=False
    )
```

```python
import functools

import jax
import jax.numpy as jnp
from jax import lax
from jax.experimental import pallas as pl
from jax.experimental.pallas import tpu as pltpu
from jax.sharding import PartitionSpec as P

MESH = pl.DeviceIdType.MESH
F32, BF16 = jnp.float32, jnp.bfloat16
NT = (((1,), (1,)), ((), ()))
TN = (((0,), (0,)), ((), ()))


def gelu_tanh(value):
    return jax.nn.gelu(value, approximate=True)


def activate(pre, act_grad):
    act, back = jax.vjp(gelu_tanh, pre)
    pre_grad = back(act_grad)[0].astype(BF16)
    return (act.astype(BF16), pre_grad)


def gelu_and_slope(x):
    c = 0.7978845608028654
    t = jnp.tanh(c * (x + 0.044715 * (x * x * x)))
    half = 0.5 * (1.0 + t)
    slope = half + 0.5 * x * (1.0 - t * t) * (c * (1.0 + 3 * 0.044715 * (x * x)))
    return x * half, slope


def exchange(
    R, N, L, wc,
    x_hbm, g_hbm, w1_hbm, w2_hbm,
    rows_x, rows_g, act_o, pg_o, in_o,
    w1, w2, own, gat, stage, part_s, part_r, ap, pgp, fpart, qpart, qrow, srow, rrow,
    w_sem, own_sem, z_send, z_recv, c_send, c_recv, r_send, r_recv, a_send, a_recv,
    h_send, h_recv, s_send, s_recv,
):
    rep, node, loc = lax.axis_index("rep"), lax.axis_index("node"), lax.axis_index("local")
    G = N * L
    b, d = x_hbm.shape
    h = w1_hbm.shape[1]
    T = G * b
    rr = T // R
    other = 1 - node
    n1 = d // wc
    hh = h // 2
    nh = hh // wc

    w1c, w2c = [], []
    for i in range(n1):
        cp = pltpu.make_async_copy(w1_hbm.at[pl.ds(i * wc, wc)], w1.at[pl.ds(i * wc, wc)], w_sem.at[0, i])
        w1c.append(cp)
    for i in range(h // wc):
        cp = pltpu.make_async_copy(w2_hbm.at[pl.ds(i * wc, wc)], w2.at[pl.ds(i * wc, wc)], w_sem.at[1, i])
        w2c.append(cp)
    oc = [
        pltpu.make_async_copy(x_hbm, own.at[0], own_sem.at[0]),
        pltpu.make_async_copy(g_hbm, own.at[1], own_sem.at[1]),
    ]
    for cp in oc + w1c[:n1 // 2]:
        cp.start()

    barrier = pltpu.get_barrier_semaphore()
    for k in range(1, L):
        pl.semaphore_signal(barrier, inc=1, device_id={"local": lax.rem(loc + k, L)}, device_id_type=MESH)
    pl.semaphore_signal(barrier, inc=1, device_id={"node": other}, device_id_type=MESH)
    for k in range(1, R):
        pl.semaphore_signal(barrier, inc=1, device_id={"rep": lax.rem(rep + k, R)}, device_id_type=MESH)
    pl.semaphore_wait(barrier, (L - 1) + 1 + (R - 1))

    mine = node * L + loc
    sends = []

    def zcopy(a, k):
        to = lax.rem(loc + k, L)
        return pltpu.make_async_remote_copy(
            src_ref=own.at[a], dst_ref=gat.at[a, mine],
            send_sem=z_send.at[a, k], recv_sem=z_recv.at[a, k],
            device_id={"local": to}, device_id_type=MESH)

    def ccopy(a, k, src, slot):
        return pltpu.make_async_remote_copy(
            src_ref=src, dst_ref=gat.at[a, slot],
            send_sem=c_send.at[a, k], recv_sem=c_recv.at[a, k],
            device_id={"node": other}, device_id_type=MESH)

    fwd = [[None] * L for _ in range(2)]
    zs = [[None] * L for _ in range(2)]

    def spread(a):
        for k in range(1, L):
            zs[a][k] = zcopy(a, k)
            zs[a][k].start()
        fwd[a][0] = ccopy(a, 0, own.at[a], mine)
        fwd[a][0].start()

    for cp in oc:
        cp.wait()
    spread(0)
    for cp in w1c[n1 // 2:]:
        cp.start()

    def gather(a):
        for k in range(1, L):
            frm = lax.rem(loc + L - k, L)
            zs[a][k].wait_recv()
            slot = node * L + frm
            fwd[a][k] = ccopy(a, k, gat.at[a, slot], slot)
            fwd[a][k].start()
        if a == 0:
            spread(1)
            for cp in w2c:
                cp.start()
        for k in range(L):
            fwd[a][k].wait_recv()
        gat[a, mine] = own[a]
        for i in range(G):
            stage[i * b:(i + 1) * b, :] = gat[a, i].astype(F32)
        return stage[...].astype(BF16)

    def rsend(a, q):
        cps = []
        for k in range(1, R):
            to = lax.rem(rep + k, R)
            cp = pltpu.make_async_remote_copy(
                src_ref=part_s.at[a, to, :, pl.ds(q * hh, hh)], dst_ref=part_r.at[a, k, :, pl.ds(q * hh, hh)],
                send_sem=r_send.at[2 * a + q, k], recv_sem=r_recv.at[2 * a + q, k],
                device_id={"rep": to}, device_id_type=MESH)
            cp.start()
            cps.append(cp)
        return cps

    rows_x[...] = gather(0)
    for cp in w1c:
        cp.wait()

    rs0, rs1 = [], []
    for q in range(2):

        @pl.loop(q * nh, (q + 1) * nh)
        def _(i):
            cols = pl.ds(pl.multiple_of(i * wc, wc), wc)
            p = jnp.dot(rows_x[...], w1[:, cols], preferred_element_type=F32)
            fpart[0, :, cols] = p
            for r in range(R):
                part_s[0, r, :, cols] = p[r * rr:(r + 1) * rr].astype(BF16)

        rs0.append(rsend(0, q))

    rows_g[...] = gather(1)
    for q in range(2):

        @pl.loop(q * nh, (q + 1) * nh)
        def _(i):
            cols = pl.ds(pl.multiple_of(i * wc, wc), wc)
            pltpu.make_async_copy(w2_hbm.at[cols], w2.at[cols], w_sem.at[1, i]).wait()
            p = lax.dot_general(rows_g[...], w2[cols, :], NT, preferred_element_type=F32)
            fpart[1, :, cols] = p
            for r in range(R):
                part_s[1, r, :, cols] = p[r * rr:(r + 1) * rr].astype(BF16)

        rs1.append(rsend(1, q))

    myrows = pl.ds(pl.multiple_of(rep * rr, rr), rr)

    def total(a, cols):
        s = fpart[a, myrows, cols]
        for k in range(1, R):
            s = s + part_r[a, k, :, cols].astype(F32)
        return s

    def asend(a, q, cols):
        cps = []
        for k in range(1, R):
            to = lax.rem(rep + k, R)
            cp = pltpu.make_async_remote_copy(
                src_ref=ap.at[a, :, cols], dst_ref=pgp.at[a, rep, :, cols],
                send_sem=a_send.at[q, k], recv_sem=a_recv.at[q, k],
                device_id={"rep": to}, device_id_type=MESH)
            cp.start()
            cps.append(cp)
        return cps

    halves = [pl.ds(q * hh, hh) for q in range(2)]
    for q, cols in enumerate(halves):
        for cp in rs0[q]:
            cp.wait_recv()
        act, slope = gelu_and_slope(total(0, cols))
        ap[0, :, cols] = act.astype(BF16)
        fpart[0, myrows, cols] = slope
    ag_pg = []
    for q, cols in enumerate(halves):
        for cp in rs1[q]:
            cp.wait_recv()
        ap[1, :, cols] = (total(1, cols) * fpart[0, myrows, cols]).astype(BF16)
        ag_pg.append(asend(1, q, cols))
        pgp[1, rep, :, cols] = ap[1, :, cols]

    def collect(q):
        for cp in ag_pg[q]:
            cp.wait_recv()
        for r in range(R):
            pg_o[r * rr:(r + 1) * rr, halves[q]] = pgp[1, r, :, halves[q]]

    hr = L * b

    C = h_send.shape[0]
    dc = d // C
    give = pl.ds(pl.multiple_of(other * hr, hr), hr)
    hx, ss = [], []

    def pass_on(c):
        cols = slice(c * dc, (c + 1) * dc)
        hx[c].wait_recv()
        for l in range(L):
            srow[l, :, cols] = (
                qpart[pl.ds(pl.multiple_of(node * hr + l * b, b), b), cols] + qrow[l * b:(l + 1) * b, cols]
            ).astype(BF16)
        for k in range(1, L):
            to = lax.rem(loc + k, L)
            cp = pltpu.make_async_remote_copy(
                src_ref=srow.at[to, :, pl.ds(c * dc, dc)], dst_ref=rrow.at[k, :, pl.ds(c * dc, dc)],
                send_sem=s_send.at[k, c], recv_sem=s_recv.at[k, c],
                device_id={"local": to}, device_id_type=MESH)
            cp.start()
            ss.append(cp)

    collect(0)
    for c in range(C):
        cols = slice(c * dc, (c + 1) * dc)
        qpart[:, cols] = lax.dot_general(pg_o[:, :hh], w1[cols, :hh], NT, preferred_element_type=F32)
    collect(1)
    ag_act = asend(0, 2, pl.ds(0, h))
    for c in range(C):
        cols = slice(c * dc, (c + 1) * dc)
        qpart[:, cols] += lax.dot_general(pg_o[:, hh:], w1[cols, hh:], NT, preferred_element_type=F32)
        cp = pltpu.make_async_remote_copy(
            src_ref=qpart.at[give, pl.ds(c * dc, dc)], dst_ref=qrow.at[:, pl.ds(c * dc, dc)],
            send_sem=h_send.at[c], recv_sem=h_recv.at[c], device_id={"node": other}, device_id_type=MESH)
        cp.start()
        hx.append(cp)
        if c:
            pass_on(c - 1)
    pass_on(C - 1)
    pgp[0, rep] = ap[0]
    for cp in ag_act:
        cp.wait_recv()
    for r in range(R):
        act_o[r * rr:(r + 1) * rr, :] = pgp[0, r]
    off = pl.multiple_of(loc * b, b)
    s = qpart[pl.ds(pl.multiple_of(node * hr + loc * b, b), b), :] + qrow[pl.ds(off, b), :]
    for cp in ss:
        cp.wait_recv()
    for k in range(1, L):
        s = s + rrow[k].astype(F32)
    in_o[...] = s.astype(BF16)
    for a in range(2):
        for k in range(1, L):
            zs[a][k].wait_send()
        for k in range(L):
            fwd[a][k].wait_send()
    for cp in rs0[0] + rs0[1] + rs1[0] + rs1[1] + ag_pg[0] + ag_pg[1] + ag_act + hx + ss:
        cp.wait_send()


def weight_grads(factor, x, pg, act, g, ing, o1, o2, o3):
    o3[...] = ing[...]
    o1[...] = lax.dot_general(x[...], pg[...], TN, preferred_element_type=F32) * factor
    o2[...] = lax.dot_general(act[...], g[...], TN, preferred_element_type=F32) * factor


def fused(R, N, L, inputs, out_grad, w_in, w_out):
    b, d = inputs.shape
    h = w_in.shape[1]
    G = N * L
    T = G * b
    rr = T // R
    wc = 256
    vm = pl.BlockSpec(memory_space=pltpu.VMEM)
    hbm = pl.BlockSpec(memory_space=pl.ANY)
    dma = pltpu.SemaphoreType.DMA
    rows_x, rows_g, act, pg, ing = pl.pallas_call(
        functools.partial(exchange, R, N, L, wc),
        out_shape=[
            jax.ShapeDtypeStruct((T, d), BF16),
            jax.ShapeDtypeStruct((T, d), BF16),
            jax.ShapeDtypeStruct((T, h), BF16),
            jax.ShapeDtypeStruct((T, h), BF16),
            jax.ShapeDtypeStruct((b, d), BF16),
        ],
        in_specs=[hbm] * 4,
        out_specs=[vm] * 5,
        scratch_shapes=[
            pltpu.VMEM((d, h), BF16),
            pltpu.VMEM((h, d), BF16),
            pltpu.VMEM((2, b, d), BF16),
            pltpu.VMEM((2, G, b, d), BF16),
            pltpu.VMEM((T, d), F32),
            pltpu.VMEM((2, R, rr, h), BF16),
            pltpu.VMEM((2, R, rr, h), BF16),
            pltpu.VMEM((2, rr, h), BF16),
            pltpu.VMEM((2, R, rr, h), BF16),
            pltpu.VMEM((2, T, h), F32),
            pltpu.VMEM((T, d), F32),
            pltpu.VMEM((L * b, d), F32),
            pltpu.VMEM((L, b, d), BF16),
            pltpu.VMEM((L, b, d), BF16),
            dma((2, max(d, h) // wc)),
            dma((2,)),
            dma((2, L)), dma((2, L)),
            dma((2, L)), dma((2, L)),
            dma((4, R)), dma((4, R)),
            dma((3, R)), dma((3, R)),
            dma((5,)), dma((5,)),
            dma((L, 5)), dma((L, 5)),
        ],
        compiler_params=pltpu.CompilerParams(
            collective_id=0, has_side_effects=True, vmem_limit_bytes=56 * 2**20
        ),
        name="exchange",
    )(inputs, out_grad, w_in, w_out)
    steps = 10
    bd, bh = d // steps, h // steps
    factor = float(T) ** -0.5
    return pl.pallas_call(
        functools.partial(weight_grads, factor),
        grid=(steps,),
        out_shape=[jax.ShapeDtypeStruct((d, h), F32), jax.ShapeDtypeStruct((h, d), F32),
                   jax.ShapeDtypeStruct((b, d), BF16)],
        in_specs=[
            pl.BlockSpec((T, bd), lambda i: (0, i)),
            pl.BlockSpec((T, h), lambda i: (0, 0)),
            pl.BlockSpec((T, bh), lambda i: (0, i)),
            pl.BlockSpec((T, d), lambda i: (0, 0)),
            pl.BlockSpec((b, d), lambda i: (0, 0)),
        ],
        out_specs=[pl.BlockSpec((bd, h), lambda i: (i, 0)), pl.BlockSpec((bh, d), lambda i: (i, 0)),
                   pl.BlockSpec((b, d), lambda i: (0, 0))],
        compiler_params=pltpu.CompilerParams(vmem_limit_bytes=60 * 2**20),
        name="weight_grads",
    )(rows_x, pg, act, rows_g, ing)


def plain(inputs, out_grad, w_in, w_out):
    rows_in, rows_grad = (
        lax.all_gather(inputs, ("node", "local"), axis=0, tiled=True),
        lax.all_gather(out_grad, ("node", "local"), axis=0, tiled=True),
    )
    pre_part = jnp.dot(rows_in, w_in, preferred_element_type=F32)
    grad_part = lax.dot_general(rows_grad, w_out, NT, preferred_element_type=F32)
    pre, act_grad = lax.psum((pre_part, grad_part), "rep")
    act, pre_grad = activate(pre, act_grad)
    factor = jnp.float32(rows_in.shape[0]) ** (-0.5)
    grad_in = lax.dot_general(rows_in, pre_grad, TN, preferred_element_type=F32) * factor
    grad_out = lax.dot_general(act, rows_grad, TN, preferred_element_type=F32) * factor
    input_part = lax.dot_general(pre_grad, w_in, NT, preferred_element_type=F32)
    owned = lax.psum_scatter(input_part, ("node", "local"), scatter_dimension=0, tiled=True)
    return (grad_in, grad_out, owned.astype(BF16))


def local(R, N, L, inputs, out_grad, w_in, w_out):
    b, d = inputs.shape
    h = w_in.shape[1]
    fits = (
        N == 2 and b % 8 == 0 and d % 1280 == 0 and h % 2560 == 0
        and (N * L * b) % (16 * R) == 0 and d * h * 4 <= 28 * 2**20
    )
    if fits:
        return fused(R, N, L, inputs, out_grad, w_in, w_out)
    return plain(inputs, out_grad, w_in, w_out)


def solution(mesh):
    R, N, L = mesh.shape["rep"], mesh.shape["node"], mesh.shape["local"]
    in_specs = (
        P(("node", "local"), "rep"),
        P(("node", "local"), "rep"),
        P("rep", ("node", "local")),
        P(("node", "local"), "rep"),
    )
    out_specs = (
        P("rep", ("node", "local")),
        P(("node", "local"), "rep"),
        P(("node", "local"), "rep"),
    )
    return jax.shard_map(
        functools.partial(local, R, N, L), mesh=mesh, in_specs=in_specs, out_specs=out_specs, check_vma=False
    )
```

```python
import functools

import jax
import jax.numpy as jnp
from jax import lax
from jax.experimental import pallas as pl
from jax.experimental.pallas import tpu as pltpu
from jax.sharding import PartitionSpec as P

MESH = pl.DeviceIdType.MESH
F32, BF16 = jnp.float32, jnp.bfloat16
NT = (((1,), (1,)), ((), ()))
TN = (((0,), (0,)), ((), ()))


def gelu_tanh(value):
    return jax.nn.gelu(value, approximate=True)


def activate(pre, act_grad):
    act, back = jax.vjp(gelu_tanh, pre)
    pre_grad = back(act_grad)[0].astype(BF16)
    return (act.astype(BF16), pre_grad)


def gelu_and_slope(x):
    c = 0.7978845608028654
    t = jnp.tanh(c * (x + 0.044715 * (x * x * x)))
    half = 0.5 * (1.0 + t)
    slope = half + 0.5 * x * (1.0 - t * t) * (c * (1.0 + 3 * 0.044715 * (x * x)))
    return x * half, slope


def exchange(
    R, N, L, wc,
    x_hbm, g_hbm, w1_hbm, w2_hbm,
    rows_x, rows_g, act_o, pg_o, in_o,
    w1, w2, own, gat, stage, part_s, part_r, ap, pgp, fpart, qpart, qrow, srow, rrow,
    w_sem, own_sem, z_send, z_recv, c_send, c_recv, r_send, r_recv, a_send, a_recv,
    h_send, h_recv, s_send, s_recv,
):
    rep, node, loc = lax.axis_index("rep"), lax.axis_index("node"), lax.axis_index("local")
    G = N * L
    b, d = x_hbm.shape
    h = w1_hbm.shape[1]
    T = G * b
    rr = T // R
    other = 1 - node
    n1 = d // wc
    hh = h // 2
    nh = hh // wc

    w1c, w2c = [], []
    for i in range(n1):
        cp = pltpu.make_async_copy(w1_hbm.at[pl.ds(i * wc, wc)], w1.at[pl.ds(i * wc, wc)], w_sem.at[0, i])
        w1c.append(cp)
    for i in range(h // wc):
        cp = pltpu.make_async_copy(w2_hbm.at[pl.ds(i * wc, wc)], w2.at[pl.ds(i * wc, wc)], w_sem.at[1, i])
        w2c.append(cp)
    oc = [
        pltpu.make_async_copy(x_hbm, own.at[0], own_sem.at[0]),
        pltpu.make_async_copy(g_hbm, own.at[1], own_sem.at[1]),
    ]
    for cp in oc + w1c[:n1 // 2]:
        cp.start()

    barrier = pltpu.get_barrier_semaphore()
    for k in range(1, L):
        pl.semaphore_signal(barrier, inc=1, device_id={"local": lax.rem(loc + k, L)}, device_id_type=MESH)
    pl.semaphore_signal(barrier, inc=1, device_id={"node": other}, device_id_type=MESH)
    for k in range(1, R):
        pl.semaphore_signal(barrier, inc=1, device_id={"rep": lax.rem(rep + k, R)}, device_id_type=MESH)
    pl.semaphore_wait(barrier, (L - 1) + 1 + (R - 1))

    mine = node * L + loc
    sends = []

    def zcopy(a, k):
        to = lax.rem(loc + k, L)
        return pltpu.make_async_remote_copy(
            src_ref=own.at[a], dst_ref=gat.at[a, mine],
            send_sem=z_send.at[a, k], recv_sem=z_recv.at[a, k],
            device_id={"local": to}, device_id_type=MESH)

    def ccopy(a, k, src, slot):
        return pltpu.make_async_remote_copy(
            src_ref=src, dst_ref=gat.at[a, slot],
            send_sem=c_send.at[a, k], recv_sem=c_recv.at[a, k],
            device_id={"node": other}, device_id_type=MESH)

    fwd = [[None] * L for _ in range(2)]
    zs = [[None] * L for _ in range(2)]

    def spread(a):
        for k in range(1, L):
            zs[a][k] = zcopy(a, k)
            zs[a][k].start()
        fwd[a][0] = ccopy(a, 0, own.at[a], mine)
        fwd[a][0].start()

    for cp in oc:
        cp.wait()
    spread(0)
    for cp in w1c[n1 // 2:]:
        cp.start()

    def gather(a):
        for k in range(1, L):
            frm = lax.rem(loc + L - k, L)
            zs[a][k].wait_recv()
            slot = node * L + frm
            fwd[a][k] = ccopy(a, k, gat.at[a, slot], slot)
            fwd[a][k].start()
        if a == 0:
            spread(1)
            for cp in w2c:
                cp.start()
        for k in range(L):
            fwd[a][k].wait_recv()
        gat[a, mine] = own[a]
        for i in range(G):
            stage[i * b:(i + 1) * b, :] = gat[a, i].astype(F32)
        return stage[...].astype(BF16)

    def rsend(a, q):
        cps = []
        for k in range(1, R):
            to = lax.rem(rep + k, R)
            cp = pltpu.make_async_remote_copy(
                src_ref=part_s.at[a, to, :, pl.ds(q * hh, hh)], dst_ref=part_r.at[a, k, :, pl.ds(q * hh, hh)],
                send_sem=r_send.at[2 * a + q, k], recv_sem=r_recv.at[2 * a + q, k],
                device_id={"rep": to}, device_id_type=MESH)
            cp.start()
            cps.append(cp)
        return cps

    rows_x[...] = gather(0)
    for cp in w1c:
        cp.wait()

    rs0, rs1 = [], []
    for q in range(2):

        @pl.loop(q * nh, (q + 1) * nh)
        def _(i):
            cols = pl.ds(pl.multiple_of(i * wc, wc), wc)
            p = jnp.dot(rows_x[...], w1[:, cols], preferred_element_type=F32)
            fpart[0, :, cols] = p
            for r in range(R):
                part_s[0, r, :, cols] = p[r * rr:(r + 1) * rr].astype(BF16)

        rs0.append(rsend(0, q))

    rows_g[...] = gather(1)
    for q in range(2):

        @pl.loop(q * nh, (q + 1) * nh)
        def _(i):
            cols = pl.ds(pl.multiple_of(i * wc, wc), wc)
            pltpu.make_async_copy(w2_hbm.at[cols], w2.at[cols], w_sem.at[1, i]).wait()
            p = lax.dot_general(rows_g[...], w2[cols, :], NT, preferred_element_type=F32)
            fpart[1, :, cols] = p
            for r in range(R):
                part_s[1, r, :, cols] = p[r * rr:(r + 1) * rr].astype(BF16)

        rs1.append(rsend(1, q))

    myrows = pl.ds(pl.multiple_of(rep * rr, rr), rr)

    def total(a, cols):
        s = fpart[a, myrows, cols]
        for k in range(1, R):
            s = s + part_r[a, k, :, cols].astype(F32)
        return s

    def asend(a, q, cols):
        cps = []
        for k in range(1, R):
            to = lax.rem(rep + k, R)
            cp = pltpu.make_async_remote_copy(
                src_ref=ap.at[a, :, cols], dst_ref=pgp.at[a, rep, :, cols],
                send_sem=a_send.at[q, k], recv_sem=a_recv.at[q, k],
                device_id={"rep": to}, device_id_type=MESH)
            cp.start()
            cps.append(cp)
        return cps

    halves = [pl.ds(q * hh, hh) for q in range(2)]
    for q, cols in enumerate(halves):
        for cp in rs0[q]:
            cp.wait_recv()
        act, slope = gelu_and_slope(total(0, cols))
        ap[0, :, cols] = act.astype(BF16)
        fpart[0, myrows, cols] = slope
    ag_pg = []
    for q, cols in enumerate(halves):
        for cp in rs1[q]:
            cp.wait_recv()
        ap[1, :, cols] = (total(1, cols) * fpart[0, myrows, cols]).astype(BF16)
        ag_pg.append(asend(1, q, cols))
        pgp[1, rep, :, cols] = ap[1, :, cols]

    def collect(q):
        for cp in ag_pg[q]:
            cp.wait_recv()
        for r in range(R):
            pg_o[r * rr:(r + 1) * rr, halves[q]] = pgp[1, r, :, halves[q]]

    hr = L * b

    C = h_send.shape[0]
    dc = d // C
    give = pl.ds(pl.multiple_of(other * hr, hr), hr)
    hx, ss = [], []

    def pass_on(c):
        cols = slice(c * dc, (c + 1) * dc)
        hx[c].wait_recv()
        for l in range(L):
            srow[l, :, cols] = (
                qpart[pl.ds(pl.multiple_of(node * hr + l * b, b), b), cols] + qrow[l * b:(l + 1) * b, cols]
            ).astype(BF16)
        for k in range(1, L):
            to = lax.rem(loc + k, L)
            cp = pltpu.make_async_remote_copy(
                src_ref=srow.at[to, :, pl.ds(c * dc, dc)], dst_ref=rrow.at[k, :, pl.ds(c * dc, dc)],
                send_sem=s_send.at[k, c], recv_sem=s_recv.at[k, c],
                device_id={"local": to}, device_id_type=MESH)
            cp.start()
            ss.append(cp)

    collect(0)
    for c in range(C):
        cols = slice(c * dc, (c + 1) * dc)
        qpart[:, cols] = lax.dot_general(pg_o[:, :hh], w1[cols, :hh], NT, preferred_element_type=F32)
    collect(1)
    ag_act = asend(0, 2, pl.ds(0, h))
    for c in range(C):
        cols = slice(c * dc, (c + 1) * dc)
        qpart[:, cols] += lax.dot_general(pg_o[:, hh:], w1[cols, hh:], NT, preferred_element_type=F32)
        cp = pltpu.make_async_remote_copy(
            src_ref=qpart.at[give, pl.ds(c * dc, dc)], dst_ref=qrow.at[:, pl.ds(c * dc, dc)],
            send_sem=h_send.at[c], recv_sem=h_recv.at[c], device_id={"node": other}, device_id_type=MESH)
        cp.start()
        hx.append(cp)
        if c:
            pass_on(c - 1)
    pass_on(C - 1)
    pgp[0, rep] = ap[0]
    for cp in ag_act:
        cp.wait_recv()
    for r in range(R):
        act_o[r * rr:(r + 1) * rr, :] = pgp[0, r]
    off = pl.multiple_of(loc * b, b)
    s = qpart[pl.ds(pl.multiple_of(node * hr + loc * b, b), b), :] + qrow[pl.ds(off, b), :]
    for cp in ss:
        cp.wait_recv()
    for k in range(1, L):
        s = s + rrow[k].astype(F32)
    in_o[...] = s.astype(BF16)
    for a in range(2):
        for k in range(1, L):
            zs[a][k].wait_send()
        for k in range(L):
            fwd[a][k].wait_send()
    for cp in rs0[0] + rs0[1] + rs1[0] + rs1[1] + ag_pg[0] + ag_pg[1] + ag_act + hx + ss:
        cp.wait_send()


def weight_grads(factor, x, pg, act, g, ing, o1, o2, o3):
    o3[...] = ing[...]
    o1[...] = lax.dot_general(x[...], pg[...], TN, preferred_element_type=F32) * factor
    o2[...] = lax.dot_general(act[...], g[...], TN, preferred_element_type=F32) * factor


def fused(R, N, L, inputs, out_grad, w_in, w_out):
    b, d = inputs.shape
    h = w_in.shape[1]
    G = N * L
    T = G * b
    rr = T // R
    wc = 256
    vm = pl.BlockSpec(memory_space=pltpu.VMEM)
    hbm = pl.BlockSpec(memory_space=pl.ANY)
    dma = pltpu.SemaphoreType.DMA
    rows_x, rows_g, act, pg, ing = pl.pallas_call(
        functools.partial(exchange, R, N, L, wc),
        out_shape=[
            jax.ShapeDtypeStruct((T, d), BF16),
            jax.ShapeDtypeStruct((T, d), BF16),
            jax.ShapeDtypeStruct((T, h), BF16),
            jax.ShapeDtypeStruct((T, h), BF16),
            jax.ShapeDtypeStruct((b, d), BF16),
        ],
        in_specs=[hbm] * 4,
        out_specs=[vm] * 5,
        scratch_shapes=[
            pltpu.VMEM((d, h), BF16),
            pltpu.VMEM((h, d), BF16),
            pltpu.VMEM((2, b, d), BF16),
            pltpu.VMEM((2, G, b, d), BF16),
            pltpu.VMEM((T, d), F32),
            pltpu.VMEM((2, R, rr, h), BF16),
            pltpu.VMEM((2, R, rr, h), BF16),
            pltpu.VMEM((2, rr, h), BF16),
            pltpu.VMEM((2, R, rr, h), BF16),
            pltpu.VMEM((2, T, h), F32),
            pltpu.VMEM((T, d), F32),
            pltpu.VMEM((L * b, d), F32),
            pltpu.VMEM((L, b, d), BF16),
            pltpu.VMEM((L, b, d), BF16),
            dma((2, max(d, h) // wc)),
            dma((2,)),
            dma((2, L)), dma((2, L)),
            dma((2, L)), dma((2, L)),
            dma((4, R)), dma((4, R)),
            dma((3, R)), dma((3, R)),
            dma((5,)), dma((5,)),
            dma((L, 5)), dma((L, 5)),
        ],
        compiler_params=pltpu.CompilerParams(
            collective_id=0, has_side_effects=True, vmem_limit_bytes=56 * 2**20
        ),
        name="exchange",
    )(inputs, out_grad, w_in, w_out)
    steps = 20
    bd, bh = d // steps, h // steps
    factor = float(T) ** -0.5
    return pl.pallas_call(
        functools.partial(weight_grads, factor),
        grid=(steps,),
        out_shape=[jax.ShapeDtypeStruct((d, h), F32), jax.ShapeDtypeStruct((h, d), F32),
                   jax.ShapeDtypeStruct((b, d), BF16)],
        in_specs=[
            pl.BlockSpec((T, bd), lambda i: (0, i)),
            pl.BlockSpec((T, h), lambda i: (0, 0)),
            pl.BlockSpec((T, bh), lambda i: (0, i)),
            pl.BlockSpec((T, d), lambda i: (0, 0)),
            pl.BlockSpec((b, d), lambda i: (0, 0)),
        ],
        out_specs=[pl.BlockSpec((bd, h), lambda i: (i, 0)), pl.BlockSpec((bh, d), lambda i: (i, 0)),
                   pl.BlockSpec((b, d), lambda i: (0, 0))],
        compiler_params=pltpu.CompilerParams(vmem_limit_bytes=60 * 2**20),
        name="weight_grads",
    )(rows_x, pg, act, rows_g, ing)


def plain(inputs, out_grad, w_in, w_out):
    rows_in, rows_grad = (
        lax.all_gather(inputs, ("node", "local"), axis=0, tiled=True),
        lax.all_gather(out_grad, ("node", "local"), axis=0, tiled=True),
    )
    pre_part = jnp.dot(rows_in, w_in, preferred_element_type=F32)
    grad_part = lax.dot_general(rows_grad, w_out, NT, preferred_element_type=F32)
    pre, act_grad = lax.psum((pre_part, grad_part), "rep")
    act, pre_grad = activate(pre, act_grad)
    factor = jnp.float32(rows_in.shape[0]) ** (-0.5)
    grad_in = lax.dot_general(rows_in, pre_grad, TN, preferred_element_type=F32) * factor
    grad_out = lax.dot_general(act, rows_grad, TN, preferred_element_type=F32) * factor
    input_part = lax.dot_general(pre_grad, w_in, NT, preferred_element_type=F32)
    owned = lax.psum_scatter(input_part, ("node", "local"), scatter_dimension=0, tiled=True)
    return (grad_in, grad_out, owned.astype(BF16))


def local(R, N, L, inputs, out_grad, w_in, w_out):
    b, d = inputs.shape
    h = w_in.shape[1]
    fits = (
        N == 2 and b % 8 == 0 and d % 2560 == 0 and h % 2560 == 0
        and (N * L * b) % (16 * R) == 0 and d * h * 4 <= 28 * 2**20
    )
    if fits:
        return fused(R, N, L, inputs, out_grad, w_in, w_out)
    return plain(inputs, out_grad, w_in, w_out)


def solution(mesh):
    R, N, L = mesh.shape["rep"], mesh.shape["node"], mesh.shape["local"]
    in_specs = (
        P(("node", "local"), "rep"),
        P(("node", "local"), "rep"),
        P("rep", ("node", "local")),
        P(("node", "local"), "rep"),
    )
    out_specs = (
        P("rep", ("node", "local")),
        P(("node", "local"), "rep"),
        P(("node", "local"), "rep"),
    )
    return jax.shard_map(
        functools.partial(local, R, N, L), mesh=mesh, in_specs=in_specs, out_specs=out_specs, check_vma=False
    )
```
